32 devices in a mesh: wide: 4 (over z), narrow: 8 (over y, x, core).
Axes of the slice: x: 2, y: 2, z: 4, core: 2. Of those that a mesh axis runs over, the one named last changes fastest.
Arguments:
- current_map: int32 [32, 1], replicated, may hold values from 0 to 15
- next_map: int32 [32, 1], replicated, may hold values from 0 to 15
- slot_counts: int32 [32, 2], P(('wide', 'narrow')), may hold values from 1 to 1024, as said below
- route: int32 [32768], P(('wide', 'narrow')), may hold values from 0 to 1023
- hidden_now: bfloat16 [32768, 768], P(('wide', 'narrow')), may hold values from -6 to 6
- grad_out: bfloat16 [32768, 2048], P(('wide', 'narrow')), may hold values from -0.1875 to 0.1875
- params: float32 [16, 768, 2048], P(None, 'narrow', 'wide'), may hold values from -0.21875 to 0.21875
- momentum: float32 [16, 768, 2048], P(None, 'narrow', 'wide'), may hold values from -6 to 6
- next_pool: bfloat16 [32768, 768], P(('wide', 'narrow')), may hold values from -6 to 6
Outputs:
- new_params: float32 [16, 768, 2048], P(None, 'narrow', 'wide')
- new_momentum: float32 [16, 768, 2048], P(None, 'narrow', 'wide')
- forward_out: bfloat16 [32768, 2048], P(('wide', 'narrow'))
The draws below stay inside these ranges and needn't reach their ends.
Inputs may be any that keep to these rules, and one draw needn't show every extreme that they name: `current_map`: every expert is held by at least one slot. `next_map`: every expert is held by at least one slot. `slot_counts`: each column reaches 1024 on some slot.
All inputs are finite; a program needn't handle non-finite values.
Results may differ from the reference program's by a relative error of at most 0.0049.
Values may be sent and summed in bfloat16 or wider, within the bound.
A program may use at most 128 MiB of HBM per device.

```python
import jax
import jax.numpy as jnp
from jax import lax

D = 2048
FF = 768
TOK = 1024
SLOTS = 32
EXPERTS = 16


def draw_slot_counts(key, part):
    first = jax.random.randint(jax.random.fold_in(key, 11), (SLOTS, 2), TOK // 4, TOK + 1)
    peak = jax.random.randint(jax.random.fold_in(key, 12), (1, 2), 0, SLOTS)
    row_index = lax.broadcasted_iota(jnp.int32, (SLOTS, 2), 0)
    return jnp.where(row_index == peak, TOK, first).astype(jnp.int32)


def place_ends(values, own_key, smallest, largest):
    longest = values.shape.index(max(values.shape))
    spots = []
    for shift in (0, 1):
        where = [jax.random.randint(jax.random.fold_in(own_key, axis), (), 0, length) for axis, length in enumerate(values.shape)]
        where[longest] = (where[longest] + shift) % values.shape[longest]
        spots.append(tuple(where))
    return values.at[spots[0]].set(smallest).at[spots[1]].set(largest)


def level_of(own_key, dims, split, least, top_value):
    gain = 1.0
    for dim, blocks in split:
        steps = jax.random.uniform(jax.random.fold_in(jax.random.fold_in(own_key, 6), dim), (blocks,), jnp.float32, least / len(split), top_value / len(split))
        gain = gain * jnp.repeat(jnp.exp(steps), dims[dim] // blocks).reshape((-1,) + (1,) * (len(dims) - 1 - dim))
    return gain


def distinct(rng, rows, amount, top, lift):
    sequence = jax.random.permutation(jax.random.fold_in(rng, 1), amount)
    favour = sequence
    for power in range(3):
        favour = favour * favour // amount
    favour = favour * lift // amount
    tickets = jax.random.randint(jax.random.fold_in(rng, 2), (rows, amount), 0, 4096) + favour
    fixed_rows = jax.random.permutation(jax.random.fold_in(rng, 3), rows)[jnp.arange(amount) % rows]
    tickets = jnp.where(jnp.arange(rows)[:, None] == fixed_rows[None, :], 1 << 14, tickets)
    priority = tickets * amount + jnp.arange(amount)
    return lax.top_k(priority.astype(jnp.int32), top)[1].astype(jnp.int32)


def bell_draw(stream_key, extent, spread, limit, cuts=(), kind=jnp.bfloat16):
    values = spread * jax.random.normal(stream_key, extent, jnp.float32)
    if cuts:
        values = values * level_of(stream_key, extent, cuts, -0.22, 0.18)
    return jnp.clip(values, -limit, limit).astype(kind)


def setup_inputs(seed: int = 0) -> dict:
    seeds = jax.random.split(jax.random.key(seed), 10)
    return {
        "current_map": distinct(seeds[0], SLOTS, EXPERTS, 1, 1024),
        "next_map": distinct(seeds[1], SLOTS, EXPERTS, 1, 1024),
        "slot_counts": draw_slot_counts(jax.random.fold_in(seeds[9], 71), 0),
        "route": place_ends(jax.random.randint(seeds[3], (SLOTS * TOK,), 0, TOK), jax.random.fold_in(seeds[3], 1), 0, TOK - 1).astype(jnp.int32),
        "hidden_now": bell_draw(seeds[4], (SLOTS * TOK, FF), 1.0, 6.0, ((0, 32),)),
        "grad_out": bell_draw(seeds[5], (SLOTS * TOK, D), (TOK ** -0.5), 0.1875, ((0, 32),)),
        "params": bell_draw(seeds[6], (EXPERTS, FF, D), FF ** -0.5, 0.21875, ((1, 8), (2, 4)), jnp.float32),
        "momentum": bell_draw(seeds[7], (EXPERTS, FF, D), 1.0, 6.0, ((1, 8), (2, 4)), jnp.float32),
        "next_pool": bell_draw(seeds[8], (SLOTS * TOK, FF), 1.0, 6.0, ((0, 32),)),
    }


momentum_decay = 0.9
step_size = 0.01


def reference(current_map, next_map, slot_counts, route, hidden_now, grad_out, params, momentum, next_pool):
    slot_total = current_map.shape[0]
    hidden_blocks = hidden_now.reshape(slot_total, TOK, FF)
    grad_blocks = grad_out.reshape(slot_total, TOK, D)
    positions = jnp.arange(TOK, dtype=jnp.int32)[:, None]

    def add_slot(totals, element):
        hidden_block, grad_block, expert, live_rows = element
        masked = jnp.where(positions < live_rows, hidden_block, jnp.zeros_like(hidden_block))
        slot_grad = jnp.dot(masked.T, grad_block, preferred_element_type=jnp.float32)
        current = lax.dynamic_index_in_dim(totals, expert, 0, keepdims=False)
        return lax.dynamic_update_index_in_dim(totals, current + slot_grad, expert, 0), None

    start_sum = jnp.zeros((EXPERTS, FF, D), jnp.float32)
    result = lax.scan(add_slot, start_sum, (hidden_blocks, grad_blocks, current_map[:, 0], slot_counts[:, 0]))
    expert_grad = result[0]
    new_momentum = momentum_decay * momentum + expert_grad
    new_params = params - step_size * (expert_grad + momentum_decay * new_momentum)
    pool_blocks = next_pool.reshape(slot_total, TOK, FF)
    route_blocks = route.reshape(slot_total, TOK)

    def forward(element):
        pool_block, picked, expert, live_rows = element
        weight = lax.dynamic_index_in_dim(new_params, expert, 0, keepdims=False).astype(jnp.bfloat16)
        gathered = jnp.take(pool_block, picked, axis=0)
        product = jnp.dot(gathered, weight, preferred_element_type=jnp.float32)
        return jnp.where(positions < live_rows, product, 0.0).astype(jnp.bfloat16)

    forward_out = lax.map(forward, (pool_blocks, route_blocks, next_map[:, 0], slot_counts[:, 1]))
    return new_params, new_momentum, forward_out.reshape(slot_total * TOK, D)
```

```python
import functools

import jax
import jax.numpy as jnp
from jax import lax
from jax.experimental import pallas as pl
from jax.experimental.pallas import tpu as pltpu
from jax.sharding import PartitionSpec as P

momentum_decay = 0.9
step_size = 0.01
AXES = ("wide", "narrow")
VMEM_LIMIT = 48 * 1024 * 1024


def grad_kernel(counts, hidden, grad, out, masked):
    @pl.when(pl.program_id(0) == 0)
    def _():
        rows = lax.broadcasted_iota(jnp.int32, hidden.shape, 0)
        masked[...] = jnp.where(rows < counts[0, 0], hidden[...], jnp.zeros_like(hidden))

    out[0] = lax.dot_general(
        masked[...], grad[...], (((0,), (0,)), ((), ())), preferred_element_type=jnp.float32
    ).astype(out.dtype)


def grad_chunk(counts, hidden, grad, wide_count, width, chunk, chunks):
    tokens, hidden_width = hidden.shape
    return pl.pallas_call(
        grad_kernel,
        grid=(wide_count,),
        in_specs=[
            pl.BlockSpec(memory_space=pltpu.SMEM),
            pl.BlockSpec((tokens, hidden_width), lambda w: (0, 0)),
            pl.BlockSpec((tokens, width), lambda w: (0, w * chunks + chunk)),
        ],
        out_specs=pl.BlockSpec((1, hidden_width, width), lambda w: (w, 0, 0)),
        out_shape=jax.ShapeDtypeStruct((wide_count, hidden_width, width), jnp.bfloat16),
        scratch_shapes=[pltpu.VMEM((tokens, hidden_width), jnp.bfloat16)],
        compiler_params=pltpu.CompilerParams(vmem_limit_bytes=VMEM_LIMIT),
        cost_estimate=pl.CostEstimate(
            flops=2 * tokens * hidden_width * width * wide_count,
            bytes_accessed=2 * (tokens * hidden_width + (tokens + hidden_width) * width * wide_count),
            transcendentals=0,
        ),
        name="slot_grad",
    )(counts, hidden, grad)


def update_kernel(first, current_map, next_map, received, params, momentum, *rest):
    new_params, new_momentum, outgoing, total = rest if first else rest[2:]
    slots = received.shape[0]
    total[...] = jnp.zeros_like(total)

    def add(s, carry):
        e = current_map[s]
        total[e] = total[e] + received[s].astype(jnp.float32)
        return carry

    lax.fori_loop(0, slots, add, 0)
    grad = total[...]
    moved = momentum_decay * momentum[...] + grad
    new_momentum[...] = moved
    new_params[...] = params[...] - step_size * (grad + momentum_decay * moved)

    def pick(s, carry):
        outgoing[s] = new_params[next_map[s]].astype(outgoing.dtype)
        return carry

    lax.fori_loop(0, slots, pick, 0)


def update_chunk(current_map, next_map, received, params, momentum, before, chunk):
    slots, rows, width = received.shape
    experts = params.shape[0]
    step = rows // 2 if rows % 32 == 0 else rows
    state = pl.BlockSpec((experts, step, width), lambda r, *_: (0, r, chunk))
    block = pl.BlockSpec((slots, step, width), lambda r, *_: (0, r, 0))
    first = before is None
    return pl.pallas_call(
        functools.partial(update_kernel, first),
        grid_spec=pltpu.PrefetchScalarGridSpec(
            num_scalar_prefetch=2,
            grid=(rows // step,),
            in_specs=[block, state, state] + ([] if first else [pl.BlockSpec(memory_space=pl.ANY)] * 2),
            out_specs=[state, state, block],
            scratch_shapes=[pltpu.VMEM((experts, step, width), jnp.float32)],
        ),
        out_shape=[
            jax.ShapeDtypeStruct(params.shape, jnp.float32),
            jax.ShapeDtypeStruct(params.shape, jnp.float32),
            jax.ShapeDtypeStruct(received.shape, jnp.bfloat16),
        ],
        input_output_aliases={} if first else {5: 0, 6: 1},
        compiler_params=pltpu.CompilerParams(vmem_limit_bytes=VMEM_LIMIT),
        cost_estimate=pl.CostEstimate(
            flops=8 * slots * rows * width,
            bytes_accessed=(4 * slots + 16 * experts) * rows * width,
            transcendentals=0,
        ),
        name="momentum_step",
    )(current_map, next_map, received, params, momentum, *([] if first else before))


def forward_kernel(first, counts, rows, weight, *rest):
    out = rest[-1]
    product = jnp.dot(rows[...], weight[0], preferred_element_type=jnp.float32)
    position = lax.broadcasted_iota(jnp.int32, product.shape, 0)
    out[...] = jnp.where(position < counts[0, 1], product, 0.0).astype(out.dtype)


def forward_chunk(counts, rows, weight, before, chunk, chunks):
    wide_count, hidden_width, width = weight.shape
    tokens = rows.shape[0]
    first = before is None
    return pl.pallas_call(
        functools.partial(forward_kernel, first),
        grid=(wide_count,),
        in_specs=[
            pl.BlockSpec(memory_space=pltpu.SMEM),
            pl.BlockSpec((tokens, hidden_width), lambda w: (0, 0)),
            pl.BlockSpec((1, hidden_width, width), lambda w: (w, 0, 0)),
        ] + ([] if first else [pl.BlockSpec(memory_space=pl.ANY)]),
        out_specs=pl.BlockSpec((tokens, width), lambda w: (0, w * chunks + chunk)),
        out_shape=jax.ShapeDtypeStruct((tokens, wide_count * width * chunks), jnp.bfloat16),
        input_output_aliases={} if first else {3: 0},
        compiler_params=pltpu.CompilerParams(vmem_limit_bytes=VMEM_LIMIT),
        cost_estimate=pl.CostEstimate(
            flops=2 * tokens * hidden_width * width * wide_count,
            bytes_accessed=2 * (tokens * hidden_width + (tokens + hidden_width) * width * wide_count),
            transcendentals=0,
        ),
        name="forward_product",
    )(counts, rows, weight, *([] if first else [before]))


def exchange(blocks):
    return lax.all_to_all(blocks, AXES, split_axis=0, concat_axis=0, tiled=True)


def local(
    current_map, next_map, slot_counts, route, hidden_now, grad_out, params, momentum, next_pool
):
    wide_count = lax.axis_size("wide")
    devices = wide_count * lax.axis_size("narrow")
    rows_own, cols_own = params.shape[1:]
    hidden_width = hidden_now.shape[1]
    chunks = 4 if cols_own % 512 == 0 else 1
    width = cols_own // chunks
    current_map, next_map = current_map[:, 0], next_map[:, 0]

    received = []
    for k in range(chunks):
        pieces = grad_chunk(slot_counts, hidden_now, grad_out, wide_count, width, k, chunks)
        received.append(exchange(pieces.reshape(devices, rows_own, width)))
    next_rows = next_pool.at[route].get(mode="promise_in_bounds")
    state, weights = None, []
    for k in range(chunks):
        *state, outgoing = update_chunk(
            current_map, next_map, received[k], params, momentum, state, k
        )
        weights.append(exchange(outgoing).reshape(wide_count, hidden_width, width))
    out = None
    for k in range(chunks):
        out = forward_chunk(slot_counts, next_rows, weights[k], out, k, chunks)
    return state[0], state[1], out


def solution(mesh):
    return jax.shard_map(
        local,
        mesh=mesh,
        in_specs=(
            P(),
            P(),
            P(("wide", "narrow"), None),
            P(("wide", "narrow")),
            P(("wide", "narrow"), None),
            P(("wide", "narrow"), None),
            P(None, "narrow", "wide"),
            P(None, "narrow", "wide"),
            P(("wide", "narrow"), None),
        ),
        out_specs=(
            P(None, "narrow", "wide"),
            P(None, "narrow", "wide"),
            P(("wide", "narrow"), None),
        ),
        check_vma=False,
    )
```

```python
import functools

import jax
import jax.numpy as jnp
from jax import lax
from jax.experimental import pallas as pl
from jax.experimental.pallas import tpu as pltpu
from jax.sharding import PartitionSpec as P

momentum_decay = 0.9
step_size = 0.01
AXES = ("wide", "narrow")
VMEM_LIMIT = 48 * 1024 * 1024


def grad_kernel(counts, hidden, grad, out, masked):
    @pl.when(pl.program_id(0) == 0)
    def _():
        rows = lax.broadcasted_iota(jnp.int32, hidden.shape, 0)
        masked[...] = jnp.where(rows < counts[0, 0], hidden[...], jnp.zeros_like(hidden))

    out[0] = lax.dot_general(
        masked[...], grad[...], (((0,), (0,)), ((), ())), preferred_element_type=jnp.float32
    ).astype(out.dtype)


def grad_chunk(counts, hidden, grad, wide_count, width, chunk, chunks):
    tokens, hidden_width = hidden.shape
    return pl.pallas_call(
        grad_kernel,
        grid=(wide_count,),
        in_specs=[
            pl.BlockSpec(memory_space=pltpu.SMEM),
            pl.BlockSpec((tokens, hidden_width), lambda w: (0, 0)),
            pl.BlockSpec((tokens, width), lambda w: (0, w * chunks + chunk)),
        ],
        out_specs=pl.BlockSpec((1, hidden_width, width), lambda w: (w, 0, 0)),
        out_shape=jax.ShapeDtypeStruct((wide_count, hidden_width, width), jnp.bfloat16),
        scratch_shapes=[pltpu.VMEM((tokens, hidden_width), jnp.bfloat16)],
        compiler_params=pltpu.CompilerParams(vmem_limit_bytes=VMEM_LIMIT),
        cost_estimate=pl.CostEstimate(
            flops=2 * tokens * hidden_width * width * wide_count,
            bytes_accessed=2 * (tokens * hidden_width + (tokens + hidden_width) * width * wide_count),
            transcendentals=0,
        ),
        name="slot_grad",
    )(counts, hidden, grad)


def update_kernel(first, current_map, next_map, received, params, momentum, *rest):
    new_params, new_momentum, outgoing, total = rest if first else rest[2:]
    slots = received.shape[0]
    total[...] = jnp.zeros_like(total)

    def add(s, carry):
        e = current_map[s]
        total[e] = total[e] + received[s].astype(jnp.float32)
        return carry

    lax.fori_loop(0, slots, add, 0)
    grad = total[...]
    moved = momentum_decay * momentum[...] + grad
    new_momentum[...] = moved
    new_params[...] = params[...] - step_size * (grad + momentum_decay * moved)

    def pick(s, carry):
        outgoing[s] = new_params[next_map[s]].astype(outgoing.dtype)
        return carry

    lax.fori_loop(0, slots, pick, 0)


def update_chunk(current_map, next_map, received, params, momentum, before, chunk):
    slots, rows, width = received.shape
    experts = params.shape[0]
    step = rows // 2 if rows % 32 == 0 else rows
    state = pl.BlockSpec((experts, step, width), lambda r, *_: (0, r, chunk))
    block = pl.BlockSpec((slots, step, width), lambda r, *_: (0, r, 0))
    first = before is None
    return pl.pallas_call(
        functools.partial(update_kernel, first),
        grid_spec=pltpu.PrefetchScalarGridSpec(
            num_scalar_prefetch=2,
            grid=(rows // step,),
            in_specs=[block, state, state] + ([] if first else [pl.BlockSpec(memory_space=pl.ANY)] * 2),
            out_specs=[state, state, block],
            scratch_shapes=[pltpu.VMEM((experts, step, width), jnp.float32)],
        ),
        out_shape=[
            jax.ShapeDtypeStruct(params.shape, jnp.float32),
            jax.ShapeDtypeStruct(params.shape, jnp.float32),
            jax.ShapeDtypeStruct(received.shape, jnp.bfloat16),
        ],
        input_output_aliases={} if first else {5: 0, 6: 1},
        compiler_params=pltpu.CompilerParams(vmem_limit_bytes=VMEM_LIMIT),
        cost_estimate=pl.CostEstimate(
            flops=8 * slots * rows * width,
            bytes_accessed=(4 * slots + 16 * experts) * rows * width,
            transcendentals=0,
        ),
        name="momentum_step",
    )(current_map, next_map, received, params, momentum, *([] if first else before))


def forward_kernel(first, counts, rows, weight, *rest):
    out = rest[-1]
    product = jnp.dot(rows[...], weight[0], preferred_element_type=jnp.float32)
    position = lax.broadcasted_iota(jnp.int32, product.shape, 0)
    out[...] = jnp.where(position < counts[0, 1], product, 0.0).astype(out.dtype)


def forward_chunk(counts, rows, weight, before, chunk, chunks):
    wide_count, hidden_width, width = weight.shape
    tokens = rows.shape[0]
    first = before is None
    return pl.pallas_call(
        functools.partial(forward_kernel, first),
        grid=(wide_count,),
        in_specs=[
            pl.BlockSpec(memory_space=pltpu.SMEM),
            pl.BlockSpec((tokens, hidden_width), lambda w: (0, 0)),
            pl.BlockSpec((1, hidden_width, width), lambda w: (w, 0, 0)),
        ] + ([] if first else [pl.BlockSpec(memory_space=pl.ANY)]),
        out_specs=pl.BlockSpec((tokens, width), lambda w: (0, w * chunks + chunk)),
        out_shape=jax.ShapeDtypeStruct((tokens, wide_count * width * chunks), jnp.bfloat16),
        input_output_aliases={} if first else {3: 0},
        compiler_params=pltpu.CompilerParams(vmem_limit_bytes=VMEM_LIMIT),
        cost_estimate=pl.CostEstimate(
            flops=2 * tokens * hidden_width * width * wide_count,
            bytes_accessed=2 * (tokens * hidden_width + (tokens + hidden_width) * width * wide_count),
            transcendentals=0,
        ),
        name="forward_product",
    )(counts, rows, weight, *([] if first else [before]))


def exchange(blocks):
    return lax.all_to_all(blocks, AXES, split_axis=0, concat_axis=0, tiled=True)


def fused_kernel(
    chunks, wide_count, narrow_count,
    current_map, next_map, counts, route, hidden_hbm, grad_hbm, params_hbm, momentum_hbm, pool_hbm,
    new_params_hbm, new_momentum_hbm, out_hbm,
    hidden, grad, params, momentum, pool, next_rows, sent, received, sent_weight, weight, out,
    load_sem, grad_sem, send_sem, receive_sem, state_sem, out_sem,
):
    devices = wide_count * narrow_count
    experts, rows, cols = params.shape
    tokens = hidden.shape[0]
    width = cols // chunks
    my_wide, my_narrow = lax.axis_index("wide"), lax.axis_index("narrow")
    me = my_wide * narrow_count + my_narrow
    bf16 = jnp.bfloat16

    def peer(j):
        return (
            lax.rem(my_wide + lax.rem(j, wide_count), wide_count),
            lax.rem(my_narrow + j // wide_count, narrow_count),
        )

    def load(source, target, i):
        copy = pltpu.make_async_copy(source, target, load_sem.at[i])
        copy.start()
        return copy

    def load_grad(k, w):
        return pltpu.make_async_copy(
            grad_hbm.at[:, pl.ds(w * cols + k * width, width)],
            grad.at[k, :, pl.ds(w * width, width)],
            grad_sem.at[k, w],
        )

    hidden_load = load(hidden_hbm, hidden, 0)
    for k in range(chunks):
        for w in range(wide_count):
            load_grad(k, w).start()
    loads = [
        load(params_hbm, params, 1),
        load(momentum_hbm, momentum, 2),
        load(pool_hbm, pool, 3),
    ]

    barrier = pltpu.get_barrier_semaphore()

    def greet(j, carry):
        pl.semaphore_signal(
            barrier, inc=1, device_id=peer(j), device_id_type=pl.DeviceIdType.MESH
        )
        return carry

    lax.fori_loop(1, devices, greet, 0)

    def place(w, n):
        return pl.ds(pl.multiple_of(n * rows, rows), rows), pl.ds(pl.multiple_of(w * width, width), width)

    def exchange_start(source, target, sems):
        own = pltpu.make_async_copy(source(my_wide, my_narrow), target, sems[1])
        own.start()

        def send(j, carry):
            to = peer(j)
            pltpu.make_async_remote_copy(
                src_ref=source(*to),
                dst_ref=target,
                send_sem=sems[0],
                recv_sem=sems[1],
                device_id=to,
                device_id_type=pl.DeviceIdType.MESH,
            ).start()
            return carry

        lax.fori_loop(1, devices, send, 0)

    hidden_load.wait()
    live = lax.broadcasted_iota(jnp.int32, hidden.shape, 0) < counts[0, 0]
    hidden[...] = jnp.where(live, hidden[...], jnp.zeros(hidden.shape, bf16))

    for k in range(chunks):
        for w in range(wide_count):
            load_grad(k, w).wait()
        sent[k] = lax.dot_general(
            hidden[...], grad[k], (((0,), (0,)), ((), ())), preferred_element_type=jnp.float32
        ).astype(bf16)
        if k == 0:
            pl.semaphore_wait(barrier, devices - 1)

        def gradient_block(w, n, k=k):
            across, along = place(w, n)
            return sent.at[k, across, along]

        exchange_start(
            gradient_block, received.at[k, me], (send_sem.at[0, k], receive_sem.at[0, k])
        )

    for copy in loads:
        copy.wait()
    picked = lax.broadcasted_iota(jnp.int32, (tokens, tokens), 0) == route[...]
    next_rows[...] = lax.dot_general(
        jnp.where(picked, 1.0, 0.0).astype(bf16),
        pool[...],
        (((0,), (0,)), ((), ())),
        preferred_element_type=jnp.float32,
    ).astype(bf16)

    for k in range(chunks):
        pltpu.make_async_copy(received.at[k], received.at[k], receive_sem.at[0, k]).wait()
        here = slice(k * width, (k + 1) * width)

        def step(e, carry, k=k, here=here):
            def add(s, total):
                block = received[k, s].astype(jnp.float32)
                return total + jnp.where(current_map[s, 0] == e, block, 0.0)

            total = lax.fori_loop(0, devices, add, jnp.zeros((rows, width), jnp.float32), unroll=4)
            moved = momentum_decay * momentum[e, :, here] + total
            momentum[e, :, here] = moved
            params[e, :, here] = params[e, :, here] - step_size * (total + momentum_decay * moved)
            return carry

        lax.fori_loop(0, experts, step, 0)

        def pick(s, carry, k=k, here=here):
            sent_weight[k, s] = params[next_map[s, 0], :, here].astype(bf16)
            return carry

        lax.fori_loop(0, devices, pick, 0)

        def weight_block(w, n, k=k):
            return sent_weight.at[k, w * narrow_count + n]

        across, along = place(my_wide, my_narrow)
        exchange_start(
            weight_block, weight.at[k, across, along], (send_sem.at[1, k], receive_sem.at[1, k])
        )
    state_copies = [
        pltpu.make_async_copy(params, new_params_hbm, state_sem.at[0]),
        pltpu.make_async_copy(momentum, new_momentum_hbm, state_sem.at[1]),
    ]
    for copy in state_copies:
        copy.start()

    out_copies = []
    for k in range(chunks):
        pltpu.make_async_copy(weight.at[k], weight.at[k], receive_sem.at[1, k]).wait()
        product = jnp.dot(next_rows[...], weight[k], preferred_element_type=jnp.float32)
        position = lax.broadcasted_iota(jnp.int32, product.shape, 0)
        out[k] = jnp.where(position < counts[0, 1], product, 0.0).astype(bf16)
        for w in range(wide_count):
            copy = pltpu.make_async_copy(
                out.at[k, :, pl.ds(w * width, width)],
                out_hbm.at[:, pl.ds(w * cols + k * width, width)],
                out_sem.at[k, w],
            )
            copy.start()
            out_copies.append(copy)
    others = received.at[0, pl.ds(0, devices - 1)]
    for part in range(2):
        for k in range(chunks):
            pltpu.make_async_copy(others, others, send_sem.at[part, k]).wait()
    for copy in state_copies + out_copies:
        copy.wait()


def fused(
    current_map, next_map, slot_counts, route, hidden_now, grad_out, params, momentum, next_pool, chunks
):
    wide_count, narrow_count = lax.axis_size("wide"), lax.axis_size("narrow")
    devices = wide_count * narrow_count
    experts, rows, cols = params.shape
    tokens, hidden_width = hidden_now.shape
    width = cols // chunks
    bf16 = jnp.bfloat16
    anywhere = pl.BlockSpec(memory_space=pl.ANY)
    scalars = pl.BlockSpec(memory_space=pltpu.SMEM)
    dma = pltpu.SemaphoreType.DMA
    return pl.pallas_call(
        functools.partial(fused_kernel, chunks, wide_count, narrow_count),
        in_specs=[scalars] * 3 + [pl.BlockSpec(memory_space=pltpu.VMEM)] + [anywhere] * 5,
        out_specs=[anywhere] * 3,
        out_shape=[
            jax.ShapeDtypeStruct(params.shape, jnp.float32),
            jax.ShapeDtypeStruct(params.shape, jnp.float32),
            jax.ShapeDtypeStruct(grad_out.shape, bf16),
        ],
        scratch_shapes=[
            pltpu.VMEM(hidden_now.shape, bf16),
            pltpu.VMEM((chunks, tokens, wide_count * width), bf16),
            pltpu.VMEM(params.shape, jnp.float32),
            pltpu.VMEM(params.shape, jnp.float32),
            pltpu.VMEM(next_pool.shape, bf16),
            pltpu.VMEM(next_pool.shape, bf16),
            pltpu.VMEM((chunks, hidden_width, wide_count * width), bf16),
            pltpu.VMEM((chunks, devices, rows, width), bf16),
            pltpu.VMEM((chunks, devices, rows, width), bf16),
            pltpu.VMEM((chunks, hidden_width, wide_count * width), bf16),
            pltpu.VMEM((chunks, tokens, wide_count * width), bf16),
            dma((4,)),
            dma((chunks, wide_count)),
            dma((2, chunks)),
            dma((2, chunks)),
            dma((2,)),
            dma((chunks, wide_count)),
        ],
        compiler_params=pltpu.CompilerParams(
            collective_id=0, has_side_effects=True, vmem_limit_bytes=60 * 1024 * 1024
        ),
        cost_estimate=pl.CostEstimate(
            flops=4 * tokens * hidden_width * wide_count * cols,
            bytes_accessed=8 * tokens * hidden_width + 4 * tokens * wide_count * cols
            + 16 * experts * rows * cols,
            transcendentals=0,
        ),
        name="exchange_and_step",
    )(
        current_map, next_map, slot_counts, route.reshape(1, tokens), hidden_now, grad_out, params,
        momentum, next_pool,
    )


def local(
    current_map, next_map, slot_counts, route, hidden_now, grad_out, params, momentum, next_pool
):
    wide_count = lax.axis_size("wide")
    devices = wide_count * lax.axis_size("narrow")
    rows_own, cols_own = params.shape[1:]
    hidden_width = hidden_now.shape[1]
    chunks = 4 if cols_own % 512 == 0 else 1
    width = cols_own // chunks
    if rows_own % 16 == 0 and width % 128 == 0:
        return tuple(
            fused(
                current_map, next_map, slot_counts, route, hidden_now, grad_out, params, momentum,
                next_pool, chunks,
            )
        )
    current_map, next_map = current_map[:, 0], next_map[:, 0]

    received = []
    for k in range(chunks):
        pieces = grad_chunk(slot_counts, hidden_now, grad_out, wide_count, width, k, chunks)
        received.append(exchange(pieces.reshape(devices, rows_own, width)))
    next_rows = next_pool.at[route].get(mode="promise_in_bounds")
    state, weights = None, []
    for k in range(chunks):
        *state, outgoing = update_chunk(
            current_map, next_map, received[k], params, momentum, state, k
        )
        weights.append(exchange(outgoing).reshape(wide_count, hidden_width, width))
    out = None
    for k in range(chunks):
        out = forward_chunk(slot_counts, next_rows, weights[k], out, k, chunks)
    return state[0], state[1], out


def solution(mesh):
    return jax.shard_map(
        local,
        mesh=mesh,
        in_specs=(
            P(),
            P(),
            P(("wide", "narrow"), None),
            P(("wide", "narrow")),
            P(("wide", "narrow"), None),
            P(("wide", "narrow"), None),
            P(None, "narrow", "wide"),
            P(None, "narrow", "wide"),
            P(("wide", "narrow"), None),
        ),
        out_specs=(
            P(None, "narrow", "wide"),
            P(None, "narrow", "wide"),
            P(("wide", "narrow"), None),
        ),
        check_vma=False,
    )
```

```python
import functools

import jax
import jax.numpy as jnp
from jax import lax
from jax.experimental import pallas as pl
from jax.experimental.pallas import tpu as pltpu
from jax.sharding import PartitionSpec as P

momentum_decay = 0.9
step_size = 0.01
AXES = ("wide", "narrow")
VMEM_LIMIT = 48 * 1024 * 1024
FLIGHT = 2


def grad_kernel(counts, hidden, grad, out, masked):
    @pl.when(pl.program_id(0) == 0)
    def _():
        rows = lax.broadcasted_iota(jnp.int32, hidden.shape, 0)
        masked[...] = jnp.where(rows < counts[0, 0], hidden[...], jnp.zeros_like(hidden))

    out[0] = lax.dot_general(
        masked[...], grad[...], (((0,), (0,)), ((), ())), preferred_element_type=jnp.float32
    ).astype(out.dtype)


def grad_chunk(counts, hidden, grad, wide_count, width, chunk, chunks):
    tokens, hidden_width = hidden.shape
    return pl.pallas_call(
        grad_kernel,
        grid=(wide_count,),
        in_specs=[
            pl.BlockSpec(memory_space=pltpu.SMEM),
            pl.BlockSpec((tokens, hidden_width), lambda w: (0, 0)),
            pl.BlockSpec((tokens, width), lambda w: (0, w * chunks + chunk)),
        ],
        out_specs=pl.BlockSpec((1, hidden_width, width), lambda w: (w, 0, 0)),
        out_shape=jax.ShapeDtypeStruct((wide_count, hidden_width, width), jnp.bfloat16),
        scratch_shapes=[pltpu.VMEM((tokens, hidden_width), jnp.bfloat16)],
        compiler_params=pltpu.CompilerParams(vmem_limit_bytes=VMEM_LIMIT),
        cost_estimate=pl.CostEstimate(
            flops=2 * tokens * hidden_width * width * wide_count,
            bytes_accessed=2 * (tokens * hidden_width + (tokens + hidden_width) * width * wide_count),
            transcendentals=0,
        ),
        name="slot_grad",
    )(counts, hidden, grad)


def update_kernel(first, current_map, next_map, received, params, momentum, *rest):
    new_params, new_momentum, outgoing, total = rest if first else rest[2:]
    slots = received.shape[0]
    total[...] = jnp.zeros_like(total)

    def add(s, carry):
        e = current_map[s]
        total[e] = total[e] + received[s].astype(jnp.float32)
        return carry

    lax.fori_loop(0, slots, add, 0)
    grad = total[...]
    moved = momentum_decay * momentum[...] + grad
    new_momentum[...] = moved
    new_params[...] = params[...] - step_size * (grad + momentum_decay * moved)

    def pick(s, carry):
        outgoing[s] = new_params[next_map[s]].astype(outgoing.dtype)
        return carry

    lax.fori_loop(0, slots, pick, 0)


def update_chunk(current_map, next_map, received, params, momentum, before, chunk):
    slots, rows, width = received.shape
    experts = params.shape[0]
    step = rows // 2 if rows % 32 == 0 else rows
    state = pl.BlockSpec((experts, step, width), lambda r, *_: (0, r, chunk))
    block = pl.BlockSpec((slots, step, width), lambda r, *_: (0, r, 0))
    first = before is None
    return pl.pallas_call(
        functools.partial(update_kernel, first),
        grid_spec=pltpu.PrefetchScalarGridSpec(
            num_scalar_prefetch=2,
            grid=(rows // step,),
            in_specs=[block, state, state] + ([] if first else [pl.BlockSpec(memory_space=pl.ANY)] * 2),
            out_specs=[state, state, block],
            scratch_shapes=[pltpu.VMEM((experts, step, width), jnp.float32)],
        ),
        out_shape=[
            jax.ShapeDtypeStruct(params.shape, jnp.float32),
            jax.ShapeDtypeStruct(params.shape, jnp.float32),
            jax.ShapeDtypeStruct(received.shape, jnp.bfloat16),
        ],
        input_output_aliases={} if first else {5: 0, 6: 1},
        compiler_params=pltpu.CompilerParams(vmem_limit_bytes=VMEM_LIMIT),
        cost_estimate=pl.CostEstimate(
            flops=8 * slots * rows * width,
            bytes_accessed=(4 * slots + 16 * experts) * rows * width,
            transcendentals=0,
        ),
        name="momentum_step",
    )(current_map, next_map, received, params, momentum, *([] if first else before))


def forward_kernel(first, counts, rows, weight, *rest):
    out = rest[-1]
    product = jnp.dot(rows[...], weight[0], preferred_element_type=jnp.float32)
    position = lax.broadcasted_iota(jnp.int32, product.shape, 0)
    out[...] = jnp.where(position < counts[0, 1], product, 0.0).astype(out.dtype)


def forward_chunk(counts, rows, weight, before, chunk, chunks):
    wide_count, hidden_width, width = weight.shape
    tokens = rows.shape[0]
    first = before is None
    return pl.pallas_call(
        functools.partial(forward_kernel, first),
        grid=(wide_count,),
        in_specs=[
            pl.BlockSpec(memory_space=pltpu.SMEM),
            pl.BlockSpec((tokens, hidden_width), lambda w: (0, 0)),
            pl.BlockSpec((1, hidden_width, width), lambda w: (w, 0, 0)),
        ] + ([] if first else [pl.BlockSpec(memory_space=pl.ANY)]),
        out_specs=pl.BlockSpec((tokens, width), lambda w: (0, w * chunks + chunk)),
        out_shape=jax.ShapeDtypeStruct((tokens, wide_count * width * chunks), jnp.bfloat16),
        input_output_aliases={} if first else {3: 0},
        compiler_params=pltpu.CompilerParams(vmem_limit_bytes=VMEM_LIMIT),
        cost_estimate=pl.CostEstimate(
            flops=2 * tokens * hidden_width * width * wide_count,
            bytes_accessed=2 * (tokens * hidden_width + (tokens + hidden_width) * width * wide_count),
            transcendentals=0,
        ),
        name="forward_product",
    )(counts, rows, weight, *([] if first else [before]))


def exchange(blocks):
    return lax.all_to_all(blocks, AXES, split_axis=0, concat_axis=0, tiled=True)


def fused_kernel(
    chunks, wide_count, narrow_count,
    current_map, next_map, counts, route, hidden_hbm, grad_hbm, params_hbm, momentum_hbm, pool_hbm,
    params, momentum, out,
    hidden, grad, pool, next_rows, sent, received, sent_weight, weight,
    load_sem, grad_sem, send_sem, receive_sem,
):
    devices = wide_count * narrow_count
    experts, rows, cols = params.shape
    tokens = hidden.shape[0]
    width = cols // chunks
    my_wide, my_narrow = lax.axis_index("wide"), lax.axis_index("narrow")
    me = my_wide * narrow_count + my_narrow
    bf16 = jnp.bfloat16

    far_first = sorted(range(wide_count), key=lambda a: -min(a, wide_count - a))

    def each_peer(act):
        def around(b, carry):
            for a in far_first:
                act(lax.rem(my_wide + a, wide_count), lax.rem(my_narrow + b, narrow_count))
            return carry

        for a in far_first[:-1]:
            act(lax.rem(my_wide + a, wide_count), my_narrow)
        lax.fori_loop(1, narrow_count, around, 0)

    def load(source, target, i):
        copy = pltpu.make_async_copy(source, target, load_sem.at[i])
        copy.start()
        return copy

    def load_grad(k, w):
        return pltpu.make_async_copy(
            grad_hbm.at[:, pl.ds(w * cols + k * width, width)],
            grad.at[k, :, pl.ds(w * width, width)],
            grad_sem.at[k, w],
        )

    hidden_load = load(hidden_hbm, hidden, 0)
    for k in range(chunks):
        for w in range(wide_count):
            load_grad(k, w).start()
    loads = [
        load(params_hbm, params, 1),
        load(momentum_hbm, momentum, 2),
        load(pool_hbm, pool, 3),
    ]

    barrier = pltpu.get_barrier_semaphore()

    def greet(*to):
        pl.semaphore_signal(barrier, inc=1, device_id=to, device_id_type=pl.DeviceIdType.MESH)

    each_peer(greet)

    def place(w, n):
        return pl.ds(pl.multiple_of(n * rows, rows), rows), pl.ds(pl.multiple_of(w * width, width), width)

    def exchange_start(source, target, sems):
        own = pltpu.make_async_copy(source(my_wide, my_narrow), target, sems[1])
        own.start()

        def send(*to):
            pltpu.make_async_remote_copy(
                src_ref=source(*to),
                dst_ref=target,
                send_sem=sems[0],
                recv_sem=sems[1],
                device_id=to,
                device_id_type=pl.DeviceIdType.MESH,
            ).start()

        each_peer(send)

    hidden_load.wait()
    live = lax.broadcasted_iota(jnp.int32, hidden.shape, 0) < counts[0, 0]
    hidden[...] = jnp.where(live, hidden[...], jnp.zeros(hidden.shape, bf16))

    others = received.at[0, pl.ds(0, devices - 1)]

    def sent_out(part, k):
        pltpu.make_async_copy(others, others, send_sem.at[part, k]).wait()

    def gradient(k):
        for w in range(wide_count):
            load_grad(k, w).wait()
        sent[k] = lax.dot_general(
            hidden[...], grad[k], (((0,), (0,)), ((), ())), preferred_element_type=jnp.float32
        ).astype(bf16)

    def send_gradient(k):
        def block(w, n):
            across, along = place(w, n)
            return sent.at[k, across, along]

        exchange_start(block, received.at[k, me], (send_sem.at[0, k], receive_sem.at[0, k]))

    def update(k):
        pltpu.make_async_copy(received.at[k], received.at[k], receive_sem.at[0, k]).wait()
        here = slice(k * width, (k + 1) * width)

        def step(e, carry):
            def add(s, total):
                block = received[k, s].astype(jnp.float32)
                return total + jnp.where(current_map[0, s] == e, block, 0.0)

            total = lax.fori_loop(0, devices, add, jnp.zeros((rows, width), jnp.float32), unroll=4)
            moved = momentum_decay * momentum[e, :, here] + total
            momentum[e, :, here] = moved
            params[e, :, here] = params[e, :, here] - step_size * (total + momentum_decay * moved)
            return carry

        lax.fori_loop(0, experts, step, 0)

        def pick(s, carry):
            sent_weight[k, s] = params[next_map[0, s], :, here].astype(bf16)
            return carry

        lax.fori_loop(0, devices, pick, 0)

    def send_weight(k):
        across, along = place(my_wide, my_narrow)
        exchange_start(
            lambda w, n: sent_weight.at[k, w * narrow_count + n],
            weight.at[k, across, along],
            (send_sem.at[1, k], receive_sem.at[1, k]),
        )

    def forward(k):
        pltpu.make_async_copy(weight.at[k], weight.at[k], receive_sem.at[1, k]).wait()
        product = jnp.dot(next_rows[...], weight[k], preferred_element_type=jnp.float32)
        position = lax.broadcasted_iota(jnp.int32, product.shape, 0)
        out[k] = jnp.where(position < counts[0, 1], product, 0.0).astype(bf16)

    def gather():
        for copy in loads:
            copy.wait()
        picked = lax.broadcasted_iota(jnp.int32, (tokens, tokens), 0) == route[...]
        next_rows[...] = lax.dot_general(
            jnp.where(picked, 1.0, 0.0).astype(bf16),
            pool[...],
            (((0,), (0,)), ((), ())),
            preferred_element_type=jnp.float32,
        ).astype(bf16)

    sends = [(0, k) for k in range(chunks)] + [(1, k) for k in range(chunks)]

    def issue(i):
        if i >= FLIGHT:
            sent_out(*sends[i - FLIGHT])
        part, k = sends[i]
        (send_weight if part else send_gradient)(k)

    gradient(0)
    pl.semaphore_wait(barrier, devices - 1)
    issued = 0
    for k in range(chunks):
        if k:
            gradient(k)
        if issued < FLIGHT:
            issue(issued)
            issued += 1
    gather()
    for k in range(chunks):
        while issued < min(len(sends), k + FLIGHT):
            issue(issued)
            issued += 1
        update(k)
    for k in range(chunks):
        while issued < min(len(sends), chunks + k + FLIGHT):
            issue(issued)
            issued += 1
        forward(k)
    for part, k in sends[-FLIGHT:]:
        sent_out(part, k)


def store_kernel(
    wide_count, params, momentum, out, new_params_hbm, new_momentum_hbm, out_hbm, state_sem, out_sem
):
    chunks, width = out.shape[0], out.shape[2] // wide_count
    copies = [
        pltpu.make_async_copy(params, new_params_hbm, state_sem.at[0]),
        pltpu.make_async_copy(momentum, new_momentum_hbm, state_sem.at[1]),
    ]
    for k in range(chunks):
        for w in range(wide_count):
            copies.append(
                pltpu.make_async_copy(
                    out.at[k, :, pl.ds(w * width, width)],
                    out_hbm.at[:, pl.ds((w * chunks + k) * width, width)],
                    out_sem.at[k, w],
                )
            )
    for copy in copies:
        copy.start()
    for copy in copies:
        copy.wait()


def fused(
    current_map, next_map, slot_counts, route, hidden_now, grad_out, params, momentum, next_pool, chunks
):
    wide_count, narrow_count = lax.axis_size("wide"), lax.axis_size("narrow")
    devices = wide_count * narrow_count
    experts, rows, cols = params.shape
    tokens, hidden_width = hidden_now.shape
    width = cols // chunks
    bf16 = jnp.bfloat16
    anywhere = pl.BlockSpec(memory_space=pl.ANY)
    scalars = pl.BlockSpec(memory_space=pltpu.SMEM)
    dma = pltpu.SemaphoreType.DMA
    in_vmem = pl.BlockSpec(memory_space=pltpu.VMEM)
    results = pl.pallas_call(
        functools.partial(fused_kernel, chunks, wide_count, narrow_count),
        in_specs=[scalars] * 3 + [in_vmem] + [anywhere] * 5,
        out_specs=[in_vmem] * 3,
        out_shape=[
            pltpu.VMEM(params.shape, jnp.float32),
            pltpu.VMEM(params.shape, jnp.float32),
            pltpu.VMEM((chunks, tokens, wide_count * width), bf16),
        ],
        scratch_shapes=[
            pltpu.VMEM(hidden_now.shape, bf16),
            pltpu.VMEM((chunks, tokens, wide_count * width), bf16),
            pltpu.VMEM(next_pool.shape, bf16),
            pltpu.VMEM(next_pool.shape, bf16),
            pltpu.VMEM((chunks, hidden_width, wide_count * width), bf16),
            pltpu.VMEM((chunks, devices, rows, width), bf16),
            pltpu.VMEM((chunks, devices, rows, width), bf16),
            pltpu.VMEM((chunks, hidden_width, wide_count * width), bf16),
            dma((4,)),
            dma((chunks, wide_count)),
            dma((2, chunks)),
            dma((2, chunks)),
        ],
        compiler_params=pltpu.CompilerParams(
            collective_id=0, has_side_effects=True, vmem_limit_bytes=53 * 1024 * 1024
        ),
        cost_estimate=pl.CostEstimate(
            flops=4 * tokens * hidden_width * wide_count * cols,
            bytes_accessed=8 * tokens * hidden_width + 4 * tokens * wide_count * cols
            + 16 * experts * rows * cols,
            transcendentals=0,
        ),
        name="exchange_and_step",
    )(
        current_map.reshape(1, devices), next_map.reshape(1, devices), slot_counts,
        route.reshape(1, tokens), hidden_now, grad_out, params, momentum, next_pool,
    )
    return pl.pallas_call(
        functools.partial(store_kernel, wide_count),
        in_specs=[in_vmem] * 3,
        out_specs=[anywhere] * 3,
        out_shape=[
            jax.ShapeDtypeStruct(params.shape, jnp.float32),
            jax.ShapeDtypeStruct(params.shape, jnp.float32),
            jax.ShapeDtypeStruct(grad_out.shape, bf16),
        ],
        scratch_shapes=[dma((2,)), dma((chunks, wide_count))],
        compiler_params=pltpu.CompilerParams(vmem_limit_bytes=16 * 1024 * 1024),
        name="store_results",
    )(*results)


def local(
    current_map, next_map, slot_counts, route, hidden_now, grad_out, params, momentum, next_pool
):
    wide_count = lax.axis_size("wide")
    devices = wide_count * lax.axis_size("narrow")
    rows_own, cols_own = params.shape[1:]
    hidden_width = hidden_now.shape[1]
    chunks = 4 if cols_own % 512 == 0 else 1
    width = cols_own // chunks
    if rows_own % 16 == 0 and width % 128 == 0:
        return tuple(
            fused(
                current_map, next_map, slot_counts, route, hidden_now, grad_out, params, momentum,
                next_pool, chunks,
            )
        )
    current_map, next_map = current_map[:, 0], next_map[:, 0]

    received = []
    for k in range(chunks):
        pieces = grad_chunk(slot_counts, hidden_now, grad_out, wide_count, width, k, chunks)
        received.append(exchange(pieces.reshape(devices, rows_own, width)))
    next_rows = next_pool.at[route].get(mode="promise_in_bounds")
    state, weights = None, []
    for k in range(chunks):
        *state, outgoing = update_chunk(
            current_map, next_map, received[k], params, momentum, state, k
        )
        weights.append(exchange(outgoing).reshape(wide_count, hidden_width, width))
    out = None
    for k in range(chunks):
        out = forward_chunk(slot_counts, next_rows, weights[k], out, k, chunks)
    return state[0], state[1], out


def solution(mesh):
    return jax.shard_map(
        local,
        mesh=mesh,
        in_specs=(
            P(),
            P(),
            P(("wide", "narrow"), None),
            P(("wide", "narrow")),
            P(("wide", "narrow"), None),
            P(("wide", "narrow"), None),
            P(None, "narrow", "wide"),
            P(None, "narrow", "wide"),
            P(("wide", "narrow"), None),
        ),
        out_specs=(
            P(None, "narrow", "wide"),
            P(None, "narrow", "wide"),
            P(("wide", "narrow"), None),
        ),
        check_vma=False,
    )
```

```python
import functools

import jax
import jax.numpy as jnp
from jax import lax
from jax.experimental import pallas as pl
from jax.experimental.pallas import tpu as pltpu
from jax.sharding import PartitionSpec as P

momentum_decay = 0.9
step_size = 0.01
AXES = ("wide", "narrow")
VMEM_LIMIT = 48 * 1024 * 1024
FLIGHT = 3


def grad_kernel(counts, hidden, grad, out, masked):
    @pl.when(pl.program_id(0) == 0)
    def _():
        rows = lax.broadcasted_iota(jnp.int32, hidden.shape, 0)
        masked[...] = jnp.where(rows < counts[0, 0], hidden[...], jnp.zeros_like(hidden))

    out[0] = lax.dot_general(
        masked[...], grad[...], (((0,), (0,)), ((), ())), preferred_element_type=jnp.float32
    ).astype(out.dtype)


def grad_chunk(counts, hidden, grad, wide_count, width, chunk, chunks):
    tokens, hidden_width = hidden.shape
    return pl.pallas_call(
        grad_kernel,
        grid=(wide_count,),
        in_specs=[
            pl.BlockSpec(memory_space=pltpu.SMEM),
            pl.BlockSpec((tokens, hidden_width), lambda w: (0, 0)),
            pl.BlockSpec((tokens, width), lambda w: (0, w * chunks + chunk)),
        ],
        out_specs=pl.BlockSpec((1, hidden_width, width), lambda w: (w, 0, 0)),
        out_shape=jax.ShapeDtypeStruct((wide_count, hidden_width, width), jnp.bfloat16),
        scratch_shapes=[pltpu.VMEM((tokens, hidden_width), jnp.bfloat16)],
        compiler_params=pltpu.CompilerParams(vmem_limit_bytes=VMEM_LIMIT),
        cost_estimate=pl.CostEstimate(
            flops=2 * tokens * hidden_width * width * wide_count,
            bytes_accessed=2 * (tokens * hidden_width + (tokens + hidden_width) * width * wide_count),
            transcendentals=0,
        ),
        name="slot_grad",
    )(counts, hidden, grad)


def update_kernel(first, current_map, next_map, received, params, momentum, *rest):
    new_params, new_momentum, outgoing, total = rest if first else rest[2:]
    slots = received.shape[0]
    total[...] = jnp.zeros_like(total)

    def add(s, carry):
        e = current_map[s]
        total[e] = total[e] + received[s].astype(jnp.float32)
        return carry

    lax.fori_loop(0, slots, add, 0)
    grad = total[...]
    moved = momentum_decay * momentum[...] + grad
    new_momentum[...] = moved
    new_params[...] = params[...] - step_size * (grad + momentum_decay * moved)

    def pick(s, carry):
        outgoing[s] = new_params[next_map[s]].astype(outgoing.dtype)
        return carry

    lax.fori_loop(0, slots, pick, 0)


def update_chunk(current_map, next_map, received, params, momentum, before, chunk):
    slots, rows, width = received.shape
    experts = params.shape[0]
    step = rows // 2 if rows % 32 == 0 else rows
    state = pl.BlockSpec((experts, step, width), lambda r, *_: (0, r, chunk))
    block = pl.BlockSpec((slots, step, width), lambda r, *_: (0, r, 0))
    first = before is None
    return pl.pallas_call(
        functools.partial(update_kernel, first),
        grid_spec=pltpu.PrefetchScalarGridSpec(
            num_scalar_prefetch=2,
            grid=(rows // step,),
            in_specs=[block, state, state] + ([] if first else [pl.BlockSpec(memory_space=pl.ANY)] * 2),
            out_specs=[state, state, block],
            scratch_shapes=[pltpu.VMEM((experts, step, width), jnp.float32)],
        ),
        out_shape=[
            jax.ShapeDtypeStruct(params.shape, jnp.float32),
            jax.ShapeDtypeStruct(params.shape, jnp.float32),
            jax.ShapeDtypeStruct(received.shape, jnp.bfloat16),
        ],
        input_output_aliases={} if first else {5: 0, 6: 1},
        compiler_params=pltpu.CompilerParams(vmem_limit_bytes=VMEM_LIMIT),
        cost_estimate=pl.CostEstimate(
            flops=8 * slots * rows * width,
            bytes_accessed=(4 * slots + 16 * experts) * rows * width,
            transcendentals=0,
        ),
        name="momentum_step",
    )(current_map, next_map, received, params, momentum, *([] if first else before))


def forward_kernel(first, counts, rows, weight, *rest):
    out = rest[-1]
    product = jnp.dot(rows[...], weight[0], preferred_element_type=jnp.float32)
    position = lax.broadcasted_iota(jnp.int32, product.shape, 0)
    out[...] = jnp.where(position < counts[0, 1], product, 0.0).astype(out.dtype)


def forward_chunk(counts, rows, weight, before, chunk, chunks):
    wide_count, hidden_width, width = weight.shape
    tokens = rows.shape[0]
    first = before is None
    return pl.pallas_call(
        functools.partial(forward_kernel, first),
        grid=(wide_count,),
        in_specs=[
            pl.BlockSpec(memory_space=pltpu.SMEM),
            pl.BlockSpec((tokens, hidden_width), lambda w: (0, 0)),
            pl.BlockSpec((1, hidden_width, width), lambda w: (w, 0, 0)),
        ] + ([] if first else [pl.BlockSpec(memory_space=pl.ANY)]),
        out_specs=pl.BlockSpec((tokens, width), lambda w: (0, w * chunks + chunk)),
        out_shape=jax.ShapeDtypeStruct((tokens, wide_count * width * chunks), jnp.bfloat16),
        input_output_aliases={} if first else {3: 0},
        compiler_params=pltpu.CompilerParams(vmem_limit_bytes=VMEM_LIMIT),
        cost_estimate=pl.CostEstimate(
            flops=2 * tokens * hidden_width * width * wide_count,
            bytes_accessed=2 * (tokens * hidden_width + (tokens + hidden_width) * width * wide_count),
            transcendentals=0,
        ),
        name="forward_product",
    )(counts, rows, weight, *([] if first else [before]))


def exchange(blocks):
    return lax.all_to_all(blocks, AXES, split_axis=0, concat_axis=0, tiled=True)


def forward_block(counts, next_rows, weight):
    product = jnp.dot(next_rows[...], weight, preferred_element_type=jnp.float32)
    position = lax.broadcasted_iota(jnp.int32, product.shape, 0)
    return jnp.where(position < counts[0, 1], product, 0.0).astype(jnp.bfloat16)


def fused_kernel(
    chunks, wide_count, narrow_count,
    current_map, next_map, counts, route, hidden_hbm, grad_hbm, params_hbm, momentum_hbm, pool_hbm,
    params, momentum, out, next_rows, last_weight,
    hidden, grad, pool, sent, received, sent_weight, weight,
    load_sem, grad_sem, send_sem, receive_sem,
):
    devices = wide_count * narrow_count
    experts, rows, cols = params.shape
    tokens = hidden.shape[0]
    width = cols // chunks
    my_wide, my_narrow = lax.axis_index("wide"), lax.axis_index("narrow")
    me = my_wide * narrow_count + my_narrow
    bf16 = jnp.bfloat16

    far_first = sorted(range(wide_count), key=lambda a: -min(a, wide_count - a))

    def each_peer(act):
        def around(b, carry):
            for a in far_first:
                act(lax.rem(my_wide + a, wide_count), lax.rem(my_narrow + b, narrow_count))
            return carry

        for a in far_first[:-1]:
            act(lax.rem(my_wide + a, wide_count), my_narrow)
        lax.fori_loop(1, narrow_count, around, 0)

    def load(source, target, i):
        copy = pltpu.make_async_copy(source, target, load_sem.at[i])
        copy.start()
        return copy

    def load_grad(k, w):
        return pltpu.make_async_copy(
            grad_hbm.at[:, pl.ds(w * cols + k * width, width)],
            grad.at[k, :, pl.ds(w * width, width)],
            grad_sem.at[k, w],
        )

    hidden_load = load(hidden_hbm, hidden, 0)
    for w in range(wide_count):
        load_grad(0, w).start()

    barrier = pltpu.get_barrier_semaphore()

    def greet(*to):
        pl.semaphore_signal(barrier, inc=1, device_id=to, device_id_type=pl.DeviceIdType.MESH)

    each_peer(greet)

    def place(w, n):
        return pl.ds(pl.multiple_of(n * rows, rows), rows), pl.ds(pl.multiple_of(w * width, width), width)

    def exchange_start(source, target, sems):
        own = pltpu.make_async_copy(source(my_wide, my_narrow), target, sems[1])
        own.start()

        def send(*to):
            pltpu.make_async_remote_copy(
                src_ref=source(*to),
                dst_ref=target,
                send_sem=sems[0],
                recv_sem=sems[1],
                device_id=to,
                device_id_type=pl.DeviceIdType.MESH,
            ).start()

        each_peer(send)

    hidden_load.wait()
    live = lax.broadcasted_iota(jnp.int32, hidden.shape, 0) < counts[0, 0]
    hidden[...] = jnp.where(live, hidden[...], jnp.zeros(hidden.shape, bf16))

    others = received.at[0, pl.ds(0, devices - 1)]

    def sent_out(part, k):
        pltpu.make_async_copy(others, others, send_sem.at[part, k]).wait()

    def gradient(k):
        for w in range(wide_count):
            load_grad(k, w).wait()
        if k + 1 < chunks:
            for w in range(wide_count):
                load_grad(k + 1, w).start()
        sent[k] = lax.dot_general(
            hidden[...], grad[k], (((0,), (0,)), ((), ())), preferred_element_type=jnp.float32
        ).astype(bf16)

    def send_gradient(k):
        def block(w, n):
            across, along = place(w, n)
            return sent.at[k, across, along]

        exchange_start(block, received.at[k, me], (send_sem.at[0, k], receive_sem.at[0, k]))

    def update(k):
        pltpu.make_async_copy(received.at[k], received.at[k], receive_sem.at[0, k]).wait()
        here = slice(k * width, (k + 1) * width)

        def step(e, carry):
            def add(s, total):
                block = received[k, s].astype(jnp.float32)
                return total + jnp.where(current_map[0, s] == e, block, 0.0)

            total = lax.fori_loop(0, devices, add, jnp.zeros((rows, width), jnp.float32), unroll=4)
            moved = momentum_decay * momentum[e, :, here] + total
            momentum[e, :, here] = moved
            params[e, :, here] = params[e, :, here] - step_size * (total + momentum_decay * moved)
            return carry

        lax.fori_loop(0, experts, step, 0)

        def pick(s, carry):
            sent_weight[k, s] = params[next_map[0, s], :, here].astype(bf16)
            return carry

        lax.fori_loop(0, devices, pick, 0)

    def send_weight(k):
        across, along = place(my_wide, my_narrow)
        exchange_start(
            lambda w, n: sent_weight.at[k, w * narrow_count + n],
            weight.at[k, across, along],
            (send_sem.at[1, k], receive_sem.at[1, k]),
        )

    def forward(k):
        pltpu.make_async_copy(weight.at[k], weight.at[k], receive_sem.at[1, k]).wait()
        if k + 1 < chunks:
            out[k] = forward_block(counts, next_rows, weight[k])
        else:
            last_weight[...] = weight[k]

    def gather():
        for copy in loads:
            copy.wait()
        picked = lax.broadcasted_iota(jnp.int32, (tokens, tokens), 0) == route[...]
        next_rows[...] = lax.dot_general(
            jnp.where(picked, 1.0, 0.0).astype(bf16),
            pool[...],
            (((0,), (0,)), ((), ())),
            preferred_element_type=jnp.float32,
        ).astype(bf16)

    sends = [(0, k) for k in range(chunks)] + [(1, k) for k in range(chunks)]

    def issue(i):
        if i >= FLIGHT:
            sent_out(*sends[i - FLIGHT])
        part, k = sends[i]
        (send_weight if part else send_gradient)(k)

    gradient(0)
    pl.semaphore_wait(barrier, devices - 1)
    issued = 0
    loads = [
        load(params_hbm, params, 1),
        load(momentum_hbm, momentum, 2),
        load(pool_hbm, pool, 3),
    ]
    for k in range(chunks):
        if k:
            gradient(k)
        if issued < FLIGHT:
            issue(issued)
            issued += 1
    gather()
    for k in range(chunks):
        while issued < min(len(sends), k + FLIGHT):
            issue(issued)
            issued += 1
        update(k)
    for k in range(chunks):
        while issued < min(len(sends), chunks + k + FLIGHT):
            issue(issued)
            issued += 1
        forward(k)
    for part, k in sends[-FLIGHT:]:
        sent_out(part, k)


def store_kernel(
    wide_count,
    counts, params, momentum, out, next_rows, last_weight,
    new_params_hbm, new_momentum_hbm, out_hbm,
    last_out, state_sem, out_sem,
):
    chunks, width = out.shape[0] + 1, out.shape[2] // wide_count
    copies = [
        pltpu.make_async_copy(params, new_params_hbm, state_sem.at[0]),
        pltpu.make_async_copy(momentum, new_momentum_hbm, state_sem.at[1]),
    ]

    def store_out(k):
        source = out.at[k] if k + 1 < chunks else last_out
        return [
            pltpu.make_async_copy(
                source.at[:, pl.ds(w * width, width)],
                out_hbm.at[:, pl.ds((w * chunks + k) * width, width)],
                out_sem.at[k, w],
            )
            for w in range(wide_count)
        ]

    for k in range(chunks - 1):
        copies += store_out(k)
    for copy in copies:
        copy.start()
    last_out[...] = forward_block(counts, next_rows, last_weight[...])
    for copy in store_out(chunks - 1):
        copy.start()
        copies.append(copy)
    for copy in copies:
        copy.wait()


def fused(
    current_map, next_map, slot_counts, route, hidden_now, grad_out, params, momentum, next_pool, chunks
):
    wide_count, narrow_count = lax.axis_size("wide"), lax.axis_size("narrow")
    devices = wide_count * narrow_count
    experts, rows, cols = params.shape
    tokens, hidden_width = hidden_now.shape
    width = cols // chunks
    bf16 = jnp.bfloat16
    anywhere = pl.BlockSpec(memory_space=pl.ANY)
    scalars = pl.BlockSpec(memory_space=pltpu.SMEM)
    dma = pltpu.SemaphoreType.DMA
    in_vmem = pl.BlockSpec(memory_space=pltpu.VMEM)
    results = pl.pallas_call(
        functools.partial(fused_kernel, chunks, wide_count, narrow_count),
        in_specs=[scalars] * 3 + [in_vmem] + [anywhere] * 5,
        out_specs=[in_vmem] * 5,
        out_shape=[
            pltpu.VMEM(params.shape, jnp.float32),
            pltpu.VMEM(params.shape, jnp.float32),
            pltpu.VMEM((chunks - 1, tokens, wide_count * width), bf16),
            pltpu.VMEM(next_pool.shape, bf16),
            pltpu.VMEM((hidden_width, wide_count * width), bf16),
        ],
        scratch_shapes=[
            pltpu.VMEM(hidden_now.shape, bf16),
            pltpu.VMEM((chunks, tokens, wide_count * width), bf16),
            pltpu.VMEM(next_pool.shape, bf16),
            pltpu.VMEM((chunks, hidden_width, wide_count * width), bf16),
            pltpu.VMEM((chunks, devices, rows, width), bf16),
            pltpu.VMEM((chunks, devices, rows, width), bf16),
            pltpu.VMEM((chunks, hidden_width, wide_count * width), bf16),
            dma((4,)),
            dma((chunks, wide_count)),
            dma((2, chunks)),
            dma((2, chunks)),
        ],
        compiler_params=pltpu.CompilerParams(
            collective_id=0, has_side_effects=True, vmem_limit_bytes=52 * 1024 * 1024
        ),
        cost_estimate=pl.CostEstimate(
            flops=4 * tokens * hidden_width * wide_count * cols,
            bytes_accessed=8 * tokens * hidden_width + 4 * tokens * wide_count * cols
            + 16 * experts * rows * cols,
            transcendentals=0,
        ),
        name="exchange_and_step",
    )(
        current_map.reshape(1, devices), next_map.reshape(1, devices), slot_counts,
        route.reshape(1, tokens), hidden_now, grad_out, params, momentum, next_pool,
    )
    return pl.pallas_call(
        functools.partial(store_kernel, wide_count),
        in_specs=[scalars] + [in_vmem] * 5,
        out_specs=[anywhere] * 3,
        out_shape=[
            jax.ShapeDtypeStruct(params.shape, jnp.float32),
            jax.ShapeDtypeStruct(params.shape, jnp.float32),
            jax.ShapeDtypeStruct(grad_out.shape, bf16),
        ],
        scratch_shapes=[
            pltpu.VMEM((tokens, wide_count * width), bf16),
            dma((2,)),
            dma((chunks, wide_count)),
        ],
        compiler_params=pltpu.CompilerParams(vmem_limit_bytes=16 * 1024 * 1024),
        name="store_results",
    )(slot_counts, *results)


def local(
    current_map, next_map, slot_counts, route, hidden_now, grad_out, params, momentum, next_pool
):
    wide_count = lax.axis_size("wide")
    devices = wide_count * lax.axis_size("narrow")
    rows_own, cols_own = params.shape[1:]
    hidden_width = hidden_now.shape[1]
    chunks = 4 if cols_own % 512 == 0 else 1
    width = cols_own // chunks
    if rows_own % 16 == 0 and width % 128 == 0 and chunks > 1:
        return tuple(
            fused(
                current_map, next_map, slot_counts, route, hidden_now, grad_out, params, momentum,
                next_pool, chunks,
            )
        )
    current_map, next_map = current_map[:, 0], next_map[:, 0]

    received = []
    for k in range(chunks):
        pieces = grad_chunk(slot_counts, hidden_now, grad_out, wide_count, width, k, chunks)
        received.append(exchange(pieces.reshape(devices, rows_own, width)))
    next_rows = next_pool.at[route].get(mode="promise_in_bounds")
    state, weights = None, []
    for k in range(chunks):
        *state, outgoing = update_chunk(
            current_map, next_map, received[k], params, momentum, state, k
        )
        weights.append(exchange(outgoing).reshape(wide_count, hidden_width, width))
    out = None
    for k in range(chunks):
        out = forward_chunk(slot_counts, next_rows, weights[k], out, k, chunks)
    return state[0], state[1], out


def solution(mesh):
    return jax.shard_map(
        local,
        mesh=mesh,
        in_specs=(
            P(),
            P(),
            P(("wide", "narrow"), None),
            P(("wide", "narrow")),
            P(("wide", "narrow"), None),
            P(("wide", "narrow"), None),
            P(None, "narrow", "wide"),
            P(None, "narrow", "wide"),
            P(("wide", "narrow"), None),
        ),
        out_specs=(
            P(None, "narrow", "wide"),
            P(None, "narrow", "wide"),
            P(("wide", "narrow"), None),
        ),
        check_vma=False,
    )
```

```python
import functools

import jax
import jax.numpy as jnp
from jax import lax
from jax.experimental import pallas as pl
from jax.experimental.pallas import tpu as pltpu
from jax.sharding import PartitionSpec as P

momentum_decay = 0.9
step_size = 0.01
AXES = ("wide", "narrow")
VMEM_LIMIT = 48 * 1024 * 1024
FLIGHT = 3


def grad_kernel(counts, hidden, grad, out, masked):
    @pl.when(pl.program_id(0) == 0)
    def _():
        rows = lax.broadcasted_iota(jnp.int32, hidden.shape, 0)
        masked[...] = jnp.where(rows < counts[0, 0], hidden[...], jnp.zeros_like(hidden))

    out[0] = lax.dot_general(
        masked[...], grad[...], (((0,), (0,)), ((), ())), preferred_element_type=jnp.float32
    ).astype(out.dtype)


def grad_chunk(counts, hidden, grad, wide_count, width, chunk, chunks):
    tokens, hidden_width = hidden.shape
    return pl.pallas_call(
        grad_kernel,
        grid=(wide_count,),
        in_specs=[
            pl.BlockSpec(memory_space=pltpu.SMEM),
            pl.BlockSpec((tokens, hidden_width), lambda w: (0, 0)),
            pl.BlockSpec((tokens, width), lambda w: (0, w * chunks + chunk)),
        ],
        out_specs=pl.BlockSpec((1, hidden_width, width), lambda w: (w, 0, 0)),
        out_shape=jax.ShapeDtypeStruct((wide_count, hidden_width, width), jnp.bfloat16),
        scratch_shapes=[pltpu.VMEM((tokens, hidden_width), jnp.bfloat16)],
        compiler_params=pltpu.CompilerParams(vmem_limit_bytes=VMEM_LIMIT),
        cost_estimate=pl.CostEstimate(
            flops=2 * tokens * hidden_width * width * wide_count,
            bytes_accessed=2 * (tokens * hidden_width + (tokens + hidden_width) * width * wide_count),
            transcendentals=0,
        ),
        name="slot_grad",
    )(counts, hidden, grad)


def update_kernel(first, current_map, next_map, received, params, momentum, *rest):
    new_params, new_momentum, outgoing, total = rest if first else rest[2:]
    slots = received.shape[0]
    total[...] = jnp.zeros_like(total)

    def add(s, carry):
        e = current_map[s]
        total[e] = total[e] + received[s].astype(jnp.float32)
        return carry

    lax.fori_loop(0, slots, add, 0)
    grad = total[...]
    moved = momentum_decay * momentum[...] + grad
    new_momentum[...] = moved
    new_params[...] = params[...] - step_size * (grad + momentum_decay * moved)

    def pick(s, carry):
        outgoing[s] = new_params[next_map[s]].astype(outgoing.dtype)
        return carry

    lax.fori_loop(0, slots, pick, 0)


def update_chunk(current_map, next_map, received, params, momentum, before, chunk):
    slots, rows, width = received.shape
    experts = params.shape[0]
    step = rows // 2 if rows % 32 == 0 else rows
    state = pl.BlockSpec((experts, step, width), lambda r, *_: (0, r, chunk))
    block = pl.BlockSpec((slots, step, width), lambda r, *_: (0, r, 0))
    first = before is None
    return pl.pallas_call(
        functools.partial(update_kernel, first),
        grid_spec=pltpu.PrefetchScalarGridSpec(
            num_scalar_prefetch=2,
            grid=(rows // step,),
            in_specs=[block, state, state] + ([] if first else [pl.BlockSpec(memory_space=pl.ANY)] * 2),
            out_specs=[state, state, block],
            scratch_shapes=[pltpu.VMEM((experts, step, width), jnp.float32)],
        ),
        out_shape=[
            jax.ShapeDtypeStruct(params.shape, jnp.float32),
            jax.ShapeDtypeStruct(params.shape, jnp.float32),
            jax.ShapeDtypeStruct(received.shape, jnp.bfloat16),
        ],
        input_output_aliases={} if first else {5: 0, 6: 1},
        compiler_params=pltpu.CompilerParams(vmem_limit_bytes=VMEM_LIMIT),
        cost_estimate=pl.CostEstimate(
            flops=8 * slots * rows * width,
            bytes_accessed=(4 * slots + 16 * experts) * rows * width,
            transcendentals=0,
        ),
        name="momentum_step",
    )(current_map, next_map, received, params, momentum, *([] if first else before))


def forward_kernel(first, counts, rows, weight, *rest):
    out = rest[-1]
    product = jnp.dot(rows[...], weight[0], preferred_element_type=jnp.float32)
    position = lax.broadcasted_iota(jnp.int32, product.shape, 0)
    out[...] = jnp.where(position < counts[0, 1], product, 0.0).astype(out.dtype)


def forward_chunk(counts, rows, weight, before, chunk, chunks):
    wide_count, hidden_width, width = weight.shape
    tokens = rows.shape[0]
    first = before is None
    return pl.pallas_call(
        functools.partial(forward_kernel, first),
        grid=(wide_count,),
        in_specs=[
            pl.BlockSpec(memory_space=pltpu.SMEM),
            pl.BlockSpec((tokens, hidden_width), lambda w: (0, 0)),
            pl.BlockSpec((1, hidden_width, width), lambda w: (w, 0, 0)),
        ] + ([] if first else [pl.BlockSpec(memory_space=pl.ANY)]),
        out_specs=pl.BlockSpec((tokens, width), lambda w: (0, w * chunks + chunk)),
        out_shape=jax.ShapeDtypeStruct((tokens, wide_count * width * chunks), jnp.bfloat16),
        input_output_aliases={} if first else {3: 0},
        compiler_params=pltpu.CompilerParams(vmem_limit_bytes=VMEM_LIMIT),
        cost_estimate=pl.CostEstimate(
            flops=2 * tokens * hidden_width * width * wide_count,
            bytes_accessed=2 * (tokens * hidden_width + (tokens + hidden_width) * width * wide_count),
            transcendentals=0,
        ),
        name="forward_product",
    )(counts, rows, weight, *([] if first else [before]))


def exchange(blocks):
    return lax.all_to_all(blocks, AXES, split_axis=0, concat_axis=0, tiled=True)


def forward_block(counts, next_rows, weight):
    product = jnp.dot(next_rows[...], weight, preferred_element_type=jnp.float32)
    position = lax.broadcasted_iota(jnp.int32, product.shape, 0)
    return jnp.where(position < counts[0, 1], product, 0.0).astype(jnp.bfloat16)


def fused_kernel(
    chunks, wide_count, narrow_count,
    current_map, next_map, counts, route, hidden_hbm, grad_hbm, params_hbm, momentum_hbm, pool_hbm,
    params, momentum, out, next_rows, last_weight,
    hidden, grad, pool, sent, received, sent_weight, weight,
    load_sem, grad_sem, send_sem, receive_sem,
):
    devices = wide_count * narrow_count
    experts, rows, cols = params.shape
    tokens = hidden.shape[0]
    width = cols // chunks
    my_wide, my_narrow = lax.axis_index("wide"), lax.axis_index("narrow")
    me = my_wide * narrow_count + my_narrow
    bf16 = jnp.bfloat16

    far_first = sorted(range(wide_count), key=lambda a: -min(a, wide_count - a))

    def each_peer(act):
        def around(b, carry):
            for a in far_first:
                act(lax.rem(my_wide + a, wide_count), lax.rem(my_narrow + b, narrow_count))
            return carry

        for a in far_first[:-1]:
            act(lax.rem(my_wide + a, wide_count), my_narrow)
        lax.fori_loop(1, narrow_count, around, 0)

    def load(source, target, i):
        copy = pltpu.make_async_copy(source, target, load_sem.at[i])
        copy.start()
        return copy

    def load_grad(k, w):
        return pltpu.make_async_copy(
            grad_hbm.at[:, pl.ds(w * cols + k * width, width)],
            grad.at[k, :, pl.ds(w * width, width)],
            grad_sem.at[k, w],
        )

    hidden_load = load(hidden_hbm, hidden, 0)
    for w in range(wide_count):
        load_grad(0, w).start()

    barrier = pltpu.get_barrier_semaphore()

    def greet(*to):
        pl.semaphore_signal(barrier, inc=1, device_id=to, device_id_type=pl.DeviceIdType.MESH)

    each_peer(greet)

    def place(w, n):
        return slice(n * rows, (n + 1) * rows), slice(w * width, (w + 1) * width)

    def exchange_start(source, target, sems):
        own = pltpu.make_async_copy(source(my_wide, my_narrow), target, sems[1])
        own.start()

        def send(*to):
            pltpu.make_async_remote_copy(
                src_ref=source(*to),
                dst_ref=target,
                send_sem=sems[0],
                recv_sem=sems[1],
                device_id=to,
                device_id_type=pl.DeviceIdType.MESH,
            ).start()

        each_peer(send)

    hidden_load.wait()
    live = lax.broadcasted_iota(jnp.int32, hidden.shape, 0) < counts[0, 0]
    hidden[...] = jnp.where(live, hidden[...], jnp.zeros(hidden.shape, bf16))

    others = received.at[0, pl.ds(0, devices - 1)]

    def sent_out(part, k):
        pltpu.make_async_copy(others, others, send_sem.at[part, k]).wait()

    def gradient(k):
        for w in range(wide_count):
            load_grad(k, w).wait()
        if k + 1 < chunks:
            for w in range(wide_count):
                load_grad(k + 1, w).start()
        product = lax.dot_general(
            hidden[...], grad[k], (((0,), (0,)), ((), ())), preferred_element_type=jnp.float32
        ).astype(bf16)
        for w in range(wide_count):
            for n in range(narrow_count):
                across, along = place(w, n)
                sent[k, w * narrow_count + n] = product[across, along]

    def send_gradient(k):
        exchange_start(
            lambda w, n: sent.at[k, w * narrow_count + n],
            received.at[k, me],
            (send_sem.at[0, k], receive_sem.at[0, k]),
        )

    def update(k):
        pltpu.make_async_copy(received.at[k], received.at[k], receive_sem.at[0, k]).wait()
        here = slice(k * width, (k + 1) * width)

        def step(e, carry):
            def add(s, total):
                block = received[k, s].astype(jnp.float32)
                return total + jnp.where(current_map[0, s] == e, block, 0.0)

            total = lax.fori_loop(0, devices, add, jnp.zeros((rows, width), jnp.float32), unroll=4)
            moved = momentum_decay * momentum[e, :, here] + total
            momentum[e, :, here] = moved
            params[e, :, here] = params[e, :, here] - step_size * (total + momentum_decay * moved)
            return carry

        lax.fori_loop(0, experts, step, 0)

        def pick(s, carry):
            sent_weight[k, s] = params[next_map[0, s], :, here].astype(bf16)
            return carry

        lax.fori_loop(0, devices, pick, 0)

    def send_weight(k):
        exchange_start(
            lambda w, n: sent_weight.at[k, w * narrow_count + n],
            weight.at[k, me],
            (send_sem.at[1, k], receive_sem.at[1, k]),
        )

    def forward(k):
        pltpu.make_async_copy(weight.at[k], weight.at[k], receive_sem.at[1, k]).wait()
        for w in range(wide_count):
            for n in range(narrow_count):
                across, along = place(w, n)
                last_weight[across, along] = weight[k, w * narrow_count + n]
        if k + 1 < chunks:
            out[k] = forward_block(counts, next_rows, last_weight[...])

    def gather():
        for copy in loads:
            copy.wait()
        picked = lax.broadcasted_iota(jnp.int32, (tokens, tokens), 0) == route[...]
        next_rows[...] = lax.dot_general(
            jnp.where(picked, 1.0, 0.0).astype(bf16),
            pool[...],
            (((0,), (0,)), ((), ())),
            preferred_element_type=jnp.float32,
        ).astype(bf16)

    sends = [(0, k) for k in range(chunks)] + [(1, k) for k in range(chunks)]

    def issue(i):
        if i >= FLIGHT:
            sent_out(*sends[i - FLIGHT])
        part, k = sends[i]
        (send_weight if part else send_gradient)(k)

    gradient(0)
    pl.semaphore_wait(barrier, devices - 1)
    issued = 0
    loads = [
        load(params_hbm, params, 1),
        load(momentum_hbm, momentum, 2),
        load(pool_hbm, pool, 3),
    ]
    for k in range(chunks):
        if k:
            gradient(k)
        if issued < FLIGHT:
            issue(issued)
            issued += 1
    gather()
    for k in range(chunks):
        while issued < min(len(sends), k + FLIGHT):
            issue(issued)
            issued += 1
        update(k)
    for k in range(chunks):
        while issued < min(len(sends), chunks + k + FLIGHT):
            issue(issued)
            issued += 1
        forward(k)
    for part, k in sends[-FLIGHT:]:
        sent_out(part, k)


def store_kernel(
    wide_count,
    counts, params, momentum, out, next_rows, last_weight,
    new_params_hbm, new_momentum_hbm, out_hbm,
    last_out, state_sem, out_sem,
):
    chunks, width = out.shape[0] + 1, out.shape[2] // wide_count
    copies = [
        pltpu.make_async_copy(params, new_params_hbm, state_sem.at[0]),
        pltpu.make_async_copy(momentum, new_momentum_hbm, state_sem.at[1]),
    ]

    def store_out(k):
        source = out.at[k] if k + 1 < chunks else last_out
        return [
            pltpu.make_async_copy(
                source.at[:, pl.ds(w * width, width)],
                out_hbm.at[:, pl.ds((w * chunks + k) * width, width)],
                out_sem.at[k, w],
            )
            for w in range(wide_count)
        ]

    for k in range(chunks - 1):
        copies += store_out(k)
    for copy in copies:
        copy.start()
    last_out[...] = forward_block(counts, next_rows, last_weight[...])
    for copy in store_out(chunks - 1):
        copy.start()
        copies.append(copy)
    for copy in copies:
        copy.wait()


def fused(
    current_map, next_map, slot_counts, route, hidden_now, grad_out, params, momentum, next_pool, chunks
):
    wide_count, narrow_count = lax.axis_size("wide"), lax.axis_size("narrow")
    devices = wide_count * narrow_count
    experts, rows, cols = params.shape
    tokens, hidden_width = hidden_now.shape
    width = cols // chunks
    bf16 = jnp.bfloat16
    anywhere = pl.BlockSpec(memory_space=pl.ANY)
    scalars = pl.BlockSpec(memory_space=pltpu.SMEM)
    dma = pltpu.SemaphoreType.DMA
    in_vmem = pl.BlockSpec(memory_space=pltpu.VMEM)
    results = pl.pallas_call(
        functools.partial(fused_kernel, chunks, wide_count, narrow_count),
        in_specs=[scalars] * 3 + [in_vmem] + [anywhere] * 5,
        out_specs=[in_vmem] * 5,
        out_shape=[
            pltpu.VMEM(params.shape, jnp.float32),
            pltpu.VMEM(params.shape, jnp.float32),
            pltpu.VMEM((chunks - 1, tokens, wide_count * width), bf16),
            pltpu.VMEM(next_pool.shape, bf16),
            pltpu.VMEM((hidden_width, wide_count * width), bf16),
        ],
        scratch_shapes=[
            pltpu.VMEM(hidden_now.shape, bf16),
            pltpu.VMEM((chunks, tokens, wide_count * width), bf16),
            pltpu.VMEM(next_pool.shape, bf16),
            pltpu.VMEM((chunks, devices, rows, width), bf16),
            pltpu.VMEM((chunks, devices, rows, width), bf16),
            pltpu.VMEM((chunks, devices, rows, width), bf16),
            pltpu.VMEM((chunks, devices, rows, width), bf16),
            dma((4,)),
            dma((chunks, wide_count)),
            dma((2, chunks)),
            dma((2, chunks)),
        ],
        compiler_params=pltpu.CompilerParams(
            collective_id=0, has_side_effects=True, vmem_limit_bytes=52 * 1024 * 1024
        ),
        cost_estimate=pl.CostEstimate(
            flops=4 * tokens * hidden_width * wide_count * cols,
            bytes_accessed=8 * tokens * hidden_width + 4 * tokens * wide_count * cols
            + 16 * experts * rows * cols,
            transcendentals=0,
        ),
        name="exchange_and_step",
    )(
        current_map.reshape(1, devices), next_map.reshape(1, devices), slot_counts,
        route.reshape(1, tokens), hidden_now, grad_out, params, momentum, next_pool,
    )
    return pl.pallas_call(
        functools.partial(store_kernel, wide_count),
        in_specs=[scalars] + [in_vmem] * 5,
        out_specs=[anywhere] * 3,
        out_shape=[
            jax.ShapeDtypeStruct(params.shape, jnp.float32),
            jax.ShapeDtypeStruct(params.shape, jnp.float32),
            jax.ShapeDtypeStruct(grad_out.shape, bf16),
        ],
        scratch_shapes=[
            pltpu.VMEM((tokens, wide_count * width), bf16),
            dma((2,)),
            dma((chunks, wide_count)),
        ],
        compiler_params=pltpu.CompilerParams(vmem_limit_bytes=16 * 1024 * 1024),
        name="store_results",
    )(slot_counts, *results)


def local(
    current_map, next_map, slot_counts, route, hidden_now, grad_out, params, momentum, next_pool
):
    wide_count = lax.axis_size("wide")
    devices = wide_count * lax.axis_size("narrow")
    rows_own, cols_own = params.shape[1:]
    hidden_width = hidden_now.shape[1]
    chunks = 4 if cols_own % 512 == 0 else 1
    width = cols_own // chunks
    if rows_own % 16 == 0 and width % 128 == 0 and chunks > 1:
        return tuple(
            fused(
                current_map, next_map, slot_counts, route, hidden_now, grad_out, params, momentum,
                next_pool, chunks,
            )
        )
    current_map, next_map = current_map[:, 0], next_map[:, 0]

    received = []
    for k in range(chunks):
        pieces = grad_chunk(slot_counts, hidden_now, grad_out, wide_count, width, k, chunks)
        received.append(exchange(pieces.reshape(devices, rows_own, width)))
    next_rows = next_pool.at[route].get(mode="promise_in_bounds")
    state, weights = None, []
    for k in range(chunks):
        *state, outgoing = update_chunk(
            current_map, next_map, received[k], params, momentum, state, k
        )
        weights.append(exchange(outgoing).reshape(wide_count, hidden_width, width))
    out = None
    for k in range(chunks):
        out = forward_chunk(slot_counts, next_rows, weights[k], out, k, chunks)
    return state[0], state[1], out


def solution(mesh):
    return jax.shard_map(
        local,
        mesh=mesh,
        in_specs=(
            P(),
            P(),
            P(("wide", "narrow"), None),
            P(("wide", "narrow")),
            P(("wide", "narrow"), None),
            P(("wide", "narrow"), None),
            P(None, "narrow", "wide"),
            P(None, "narrow", "wide"),
            P(("wide", "narrow"), None),
        ),
        out_specs=(
            P(None, "narrow", "wide"),
            P(None, "narrow", "wide"),
            P(("wide", "narrow"), None),
        ),
        check_vma=False,
    )
```
